256 devices in a mesh: section: 8 (over z_hi, y), expert: 32 (over x, z_lo, core).
Axes of the slice: x: 4, y: 4, z: 8 (z_hi: 2, z_lo: 4; z = z_hi * 4 + z_lo), core: 2. Of those that a mesh axis runs over, the one named last changes fastest.
Arguments:
- rising: bfloat16 [8, 2048, 3584], P('section', 'expert'), may hold values from -6 to 6
- falling: bfloat16 [8, 2048, 3584], P('section', 'expert'), may hold values from -6 to 6
- gate_up: bfloat16 [8, 2, 2, 3584, 8192], P('section', None, None, None, 'expert'), may hold values from -0.09375 to 0.09375
- down_proj: bfloat16 [8, 2, 8192, 3584], P('section', None, 'expert'), may hold values from -0.1875 to 0.1875
- norm_gains: float32 [8, 2, 3584], P('section'), may hold values from 0.25 to 1.75
- expert_ids: int32 [8, 2, 2048, 2], P('section', None, 'expert'), may hold values from 0 to 7, all different within a row; in each aligned block of 64 rows (0 to 63, 64 to 127, ..., all dimensions but the last counted through in order) at most 20 rows name the same one
- gate_values: float32 [8, 2, 2048, 2], P('section', None, 'expert'), may hold values from 0.2 to 1
Outputs:
- rising_next: bfloat16 [8, 2048, 3584], P('section', 'expert')
- falling_next: bfloat16 [8, 2048, 3584], P('section', 'expert')
The draws below stay inside these ranges and needn't reach their ends.
Inputs may be any that keep to these rules, and one draw needn't show every extreme that they name: `expert_ids`: among the 64 tokens of one device for one section slot, no expert is chosen more than 20 times, a bound that some block reaches; a token's 2 choices differ.
All inputs are finite; a program needn't handle non-finite values.
Results may differ from the reference program's by a relative error of at most 0.0052.
Values may be sent and summed in bfloat16 or wider, within the bound.
No kernel may reach another device: no remote copies, remote signals or barrier semaphores. Data moves between devices by JAX's collectives and lax.ppermute only.
A program may use at most 128 MiB of HBM per device.

```python
import math
import jax
import jax.numpy as jnp
import numpy as np
from jax import lax

D = 3584
FFE = 1024
FFE_DEV = 256
TOP = 2
TOK = 64
SPLIT = 4
EXPERTS = 8
CAP = 20
MICRO = 2048
N_SECTION = 8
N_EXPERT = 32


def steps_of(key, dims, split, smallest, largest):
    level, own = 1.0, jax.random.fold_in(key, 6)
    for dim, shards_of in split:
        draws = jnp.exp(jax.random.uniform(jax.random.fold_in(own, dim), (shards_of,), jnp.float32, smallest / len(split), largest / len(split)))
        level = level * jnp.repeat(draws, dims[dim] // shards_of).reshape([-1 if axis == dim else 1 for axis in range(len(dims))])
    return level


def shared_out(key, own, number, rows, count, top, bound, slope):
    ranking = jax.random.permutation(key, count)
    heavy_load, common = portions_of(count, rows * top, bound, slope, True), portions_of(count, rows * top, bound, slope, False)
    places = jnp.arange(count)

    def named(tallies, offset_by):
        used = int((tallies > 0).sum())
        fixed = max(1, used // 4)
        shifted = fixed + (places - fixed + offset_by * (used - fixed)) % max(1, count - fixed)
        return jnp.zeros((count,), jnp.int32).at[ranking[jnp.where(places < fixed, places, shifted)]].set(jnp.asarray(tallies, jnp.int32))

    tallies = jnp.where(number % 4 == 0, named(heavy_load, number // 4), named(common, number - number // 4 - 1))
    mixed = jax.random.permutation(jax.random.fold_in(own, 3), count)
    source_of, sink = mixed[0:count // 2 * 2:2], mixed[1:count // 2 * 2:2]
    slack = jnp.minimum(tallies[source_of] - 1, bound - tallies[sink]) // 2
    slack = jnp.where((source_of == ranking[0]) | (sink == ranking[0]) | (tallies[sink] == 0), 0, jnp.maximum(slack, 0))
    shifted = jax.random.randint(jax.random.fold_in(own, 4), (count // 2,), 0, 1 << 20) % (slack + 1)
    tallies = tallies.at[source_of].add(-shifted).at[sink].add(shifted)
    items = jnp.searchsorted(jnp.cumsum(tallies), jnp.arange(rows * top), side="right").astype(jnp.int32)
    grid = items.reshape(top, rows).T
    grid = grid[jax.random.permutation(jax.random.fold_in(own, 1), rows)]
    offset_by = jax.random.randint(jax.random.fold_in(own, 2), (rows, 1), 0, top)
    return jnp.take_along_axis(grid, (jnp.arange(top)[None, :] + offset_by) % top, axis=1)


def portions_of(amount, total, bound, skew, full):
    loads = [(1 << 20) // math.isqrt(grade ** skew) + 1 for grade in range(1, amount + 1)]
    largest = bound if full else min(bound, max(-(-total // amount), total * loads[0] // sum(loads)))
    least = 1 if total - largest >= amount - 1 else 0
    counts, surplus = [largest] + [least] * (amount - 1), total - largest - least * (amount - 1)
    while surplus > 0:
        movable = [i for i in range(1, amount) if counts[i] < largest] or [i for i in range(1, amount) if counts[i] < bound]
        mass, left = sum([loads[i] for i in movable]), surplus
        for i in movable:
            addition = min(bound - counts[i], max(1, left * loads[i] // mass), surplus)
            counts[i] = counts[i] + addition
            surplus = surplus - addition
    return np.array(counts)


def bell_draw(rng, shape, width, reach, shards=(), kind=jnp.bfloat16):
    loudness = steps_of(rng, shape, shards, -0.22, 0.18) if shards else 1.0
    values = jax.random.normal(rng, shape, jnp.float32) * width * loudness
    return jnp.minimum(jnp.maximum(values, -reach), reach).astype(kind)


def setup_inputs(seed: int = 0) -> dict:
    splits = jax.random.split(jax.random.key(seed), 8)
    rising = bell_draw(splits[0], (N_SECTION, MICRO, D), 1.0, 6.0, ((0, 8), (1, 32)))
    falling = bell_draw(splits[1], (N_SECTION, MICRO, D), 1.0, 6.0, ((0, 8), (1, 32)))
    gate_up = bell_draw(splits[2], (N_SECTION, 2, 2, D, EXPERTS * FFE), D ** -0.5, 0.09375, ((0, 8), (4, 32)))
    down_proj = bell_draw(splits[3], (N_SECTION, 2, EXPERTS * FFE, D), FFE ** -0.5, 0.1875, ((0, 8), (2, 32)))
    norm_gains = jnp.clip(1.0 + 0.15 * jax.random.normal(splits[4], (N_SECTION, 2, D), jnp.float32), 0.25, 1.75)
    expert_ids_keys = jax.random.split(jax.random.fold_in(splits[5], 1), N_SECTION * 2 * MICRO // TOK)
    expert_ids_turns = jax.random.permutation(jax.random.fold_in(splits[5], 3), N_SECTION * 2 * MICRO // TOK)
    expert_ids = jax.vmap(lambda own, number: shared_out(jax.random.fold_in(splits[5], 2), own, number, TOK, EXPERTS, TOP, CAP, 2))(expert_ids_keys, expert_ids_turns).reshape((N_SECTION, 2, MICRO, TOP))
    gate_values = jnp.clip(0.2 + 0.8 * jax.random.uniform(splits[6], (N_SECTION, 2, MICRO, TOP), jnp.float32) ** steps_of(splits[6], (N_SECTION, 2, MICRO, TOP), ((0, 8), (2, 32)), -0.2, 0.2), 0.2, 1.0)
    return dict(rising=rising, falling=falling, gate_up=gate_up, down_proj=down_proj, norm_gains=norm_gains, expert_ids=expert_ids, gate_values=gate_values)


EPSILON = 1e-06

def rms_norm(values, gain_row):
    as_float = values.astype(jnp.float32)
    scale = lax.rsqrt(lax.optimization_barrier(jnp.mean(as_float * as_float, axis=-1, keepdims=True)) + EPSILON)
    return (as_float * scale * gain_row).astype(jnp.bfloat16)

def slot_index(routes, experts, capacity):
    flat_ids = routes.reshape(-1)
    onehot = (flat_ids[:, None] == jnp.arange(experts, dtype=jnp.int32)[None, :]).astype(jnp.int32)
    position = jnp.cumsum(onehot, axis=0) - 1
    return (flat_ids * capacity + lax.optimization_barrier(jnp.sum(position * onehot, axis=1))).astype(jnp.int32)

def dispatch_rows(normed, slot_ids, slots, top_count):
    paired = slot_ids.reshape(-1, top_count)
    one_hot = lax.optimization_barrier(jnp.sum((paired[None, :, :] == jnp.arange(slots, dtype=jnp.int32)[:, None, None]).astype(jnp.float32), axis=2))
    return jnp.dot(one_hot.astype(jnp.bfloat16), normed, preferred_element_type=jnp.float32).astype(jnp.bfloat16)

def moe_layer(values, gain_row, gate_up, down_proj, routes, gate_values):
    blocks = values.reshape(N_EXPERT, TOK, D)
    normed = rms_norm(blocks, gain_row)
    slot_ids = jax.vmap(lambda chosen: slot_index(chosen, EXPERTS, CAP))(routes.reshape(N_EXPERT, TOK, TOP))
    buffer = jax.vmap(lambda rows_in, slots_in: dispatch_rows(rows_in, slots_in, EXPERTS * CAP, TOP))(normed, slot_ids)
    buffer = buffer.reshape(N_EXPERT, EXPERTS, CAP, D)

    def expert_out(expert):
        flat_rows = lax.dynamic_index_in_dim(buffer, expert, 1, keepdims=False).reshape(-1, D)
        running = jnp.zeros((N_EXPERT * CAP, D), jnp.float32)
        for shard in range(SPLIT):
            column = expert * FFE + shard * FFE_DEV
            gate_out = jnp.dot(flat_rows, lax.dynamic_slice_in_dim(gate_up[0], column, FFE_DEV, 1), preferred_element_type=jnp.float32)
            up_out = jnp.dot(flat_rows, lax.dynamic_slice_in_dim(gate_up[1], column, FFE_DEV, 1), preferred_element_type=jnp.float32)
            hidden = (jax.nn.silu(gate_out) * up_out).astype(jnp.bfloat16)
            partial_value = jnp.dot(hidden, lax.dynamic_slice_in_dim(down_proj, column, FFE_DEV, 0), preferred_element_type=jnp.float32).astype(jnp.bfloat16)
            running = running + partial_value.astype(jnp.float32)
        return running.reshape(N_EXPERT, CAP, D)
    outputs = lax.map(expert_out, jnp.arange(EXPERTS, dtype=jnp.int32))
    summed = jnp.transpose(outputs, (1, 0, 2, 3)).reshape(N_EXPERT, EXPERTS * CAP, D)
    picked = jax.vmap(lambda table, where_at: jnp.take(table, where_at, axis=0))(summed, slot_ids)
    picked = picked.reshape(N_EXPERT, TOK, TOP, D)
    mixture = lax.optimization_barrier(jnp.sum(picked * gate_values.reshape(N_EXPERT, TOK, TOP)[..., None], axis=2))
    return (blocks.astype(jnp.float32) + mixture).astype(jnp.bfloat16).reshape(MICRO, D)

def reference(rising, falling, gate_up, down_proj, norm_gains, expert_ids, gate_values):
    low_outs = []
    high_outs = []
    for device in range(N_SECTION):
        low_outs.append(moe_layer(rising[device], norm_gains[device, 0], gate_up[device, 0], down_proj[device, 0], expert_ids[device, 0], gate_values[device, 0]))
        high_outs.append(moe_layer(falling[device], norm_gains[device, 1], gate_up[device, 1], down_proj[device, 1], expert_ids[device, 1], gate_values[device, 1]))
    low_stack = jnp.stack(low_outs)
    high_stack = jnp.stack(high_outs)
    rising_next = jnp.concatenate([high_stack[0:1], low_stack[:-1]], axis=0)
    falling_next = jnp.concatenate([high_stack[1:], low_stack[-1:]], axis=0)
    return (rising_next, falling_next)
```

```python
import functools

import jax
import jax.numpy as jnp
from jax import lax
from jax.experimental import pallas as pl
from jax.experimental.pallas import tpu as pltpu
from jax.sharding import PartitionSpec as P

EPSILON = 1e-06
X, Z, C = 4, 4, 2
CAP = 20
SENT = ((1792, 1792), (1792, 1792))
BACK = ((1792, 1792), (1792, 1792))


def moved(block, place):
    route = []
    for x in range(X):
        for z in range(Z):
            for c in range(C):
                tx, tz, tc = place(x, z, c)
                route.append(((x * Z + z) * C + c, ((tx % X) * Z + tz) * C + tc))
    return lax.ppermute(block, "expert", route)


def along_x(block, k):
    return moved(block, lambda x, z, c: (x + k, z, c))


def across_z(block, k):
    return moved(block, lambda x, z, c: (x, z ^ k, c))


def across_cores(block):
    return moved(block, lambda x, z, c: (x, z, 1 - c))


def shifted(block, distance):
    devices = range(lax.axis_size("section"))
    route = [(i, i + distance) for i in devices if i + distance in devices]
    return lax.ppermute(block, "section", route)


def starts(widths):
    return [sum(widths[:i]) for i in range(len(widths))]


def call(kernel, out_shape, flops, moved_bytes, **kw):
    return pl.pallas_call(
        kernel,
        out_shape=out_shape,
        cost_estimate=pl.CostEstimate(flops=flops, bytes_accessed=moved_bytes, transcendentals=0),
        compiler_params=pltpu.CompilerParams(vmem_limit_bytes=48 * 1024 * 1024),
        **kw,
    )


def norm(values, gain_row, widths):
    rows, width = values.shape

    def kernel(x_ref, gain_ref, *outs):
        x = x_ref[...].astype(jnp.float32)
        scale = lax.rsqrt(jnp.mean(x * x, axis=-1, keepdims=True) + EPSILON)
        normed = (x * scale * gain_ref[...]).astype(jnp.bfloat16)
        for out, at in zip(outs, starts(widths)):
            out[...] = normed[:, at : at + out.shape[1]]

    shapes = [jax.ShapeDtypeStruct((rows, w), jnp.bfloat16) for w in widths]
    return call(kernel, shapes, rows * width * 6, rows * width * 4)(values, gain_row[None])


def dispatch(one_hot, near, far, side, corner):
    slots = one_hot.shape[0] // X
    rows, width = near.shape

    def kernel(hot_ref, a, b, c, d, *outs):
        tokens = jnp.concatenate([a[...], b[...], c[...], d[...]], axis=0)
        for k in range(X):
            outs[k][...] = jnp.dot(
                hot_ref[k * slots : (k + 1) * slots], tokens, preferred_element_type=jnp.float32
            ).astype(jnp.bfloat16)

    shapes = [jax.ShapeDtypeStruct((slots, width), jnp.bfloat16)] * X
    return call(
        kernel, shapes, 2 * X * slots * Z * rows * width, (X * slots + Z * rows) * width * 2
    )(one_hot, near, far, side, corner)


def gated(parts, own, peer, slot):
    slots = parts[0][0].shape[0]
    widths = [p[0].shape[1] for p in parts]
    total, units = own.shape[3], own.shape[4]
    rows = X * slots
    tile = 896
    steps = total // tile
    flat = [b for p in parts for b in p]

    def kernel(*refs):
        blocks, (g0, u0, g1, u1, hidden, held, acc) = refs[: len(flat)], refs[len(flat) :]
        step = pl.program_id(0)

        @pl.when(step == 0)
        def _():
            acc[...] = jnp.zeros_like(acc)
            for n, (w, at) in enumerate(zip(widths, starts(widths))):
                for k in range(X):
                    for s in range(steps):
                        lo, hi = max(at, s * tile), min(at + w, (s + 1) * tile)
                        if lo < hi:
                            held[s, k * slots : (k + 1) * slots, lo - s * tile : hi - s * tile] = (
                                blocks[n * X + k][:, lo - at : hi - at]
                            )

        x = held[step]
        for n, w in enumerate((g0, u0, g1, u1)):
            acc[n] += jnp.dot(x, w[0, 0, 0], preferred_element_type=jnp.float32)

        @pl.when(step == steps - 1)
        def _():
            for n in range(C):
                gate = acc[2 * n]
                value = gate / (1.0 + jnp.exp(-gate)) * acc[2 * n + 1]
                hidden[:, n * units : (n + 1) * units] = value.astype(jnp.bfloat16)

    def weight(which):
        return pl.BlockSpec((1, 1, 1, tile, units), lambda s: (0, slot, which, s, 0))

    return call(
        kernel,
        jax.ShapeDtypeStruct((rows, C * units), jnp.bfloat16),
        2 * rows * total * C * 2 * units,
        total * C * 2 * units * 2 + rows * total * 2,
        grid=(steps,),
        in_specs=[pl.BlockSpec(b.shape, lambda s: (0, 0)) for b in flat]
        + [weight(0), weight(1), weight(0), weight(1)],
        out_specs=pl.BlockSpec((rows, C * units), lambda s: (0, 0)),
        scratch_shapes=[
            pltpu.VMEM((steps, rows, tile), jnp.bfloat16),
            pltpu.VMEM((2 * C, rows, units), jnp.float32),
        ],
    )(*flat, own, own, peer, peer)


def lowered(hidden, own, peer, slot, at, width):
    rows = hidden.shape[0]
    slots = rows // X
    units = own.shape[2]
    tile = 896
    first = at // tile

    def kernel(hidden_ref, w0, w1, *outs):
        value = jnp.dot(hidden_ref[:, :units], w0[0, 0], preferred_element_type=jnp.float32)
        value += jnp.dot(hidden_ref[:, units:], w1[0, 0], preferred_element_type=jnp.float32)
        for k in range(X):
            outs[k][...] = value[k * slots : (k + 1) * slots].astype(jnp.bfloat16)

    weight = pl.BlockSpec((1, 1, units, tile), lambda s: (0, slot, 0, first + s))
    return call(
        kernel,
        [jax.ShapeDtypeStruct((slots, width), jnp.bfloat16)] * X,
        2 * rows * C * units * width,
        (C * units + rows) * width * 2,
        grid=(width // tile,),
        in_specs=[pl.BlockSpec(hidden.shape, lambda s: (0, 0)), weight, weight],
        out_specs=[pl.BlockSpec((slots, tile), lambda s: (0, s))] * X,
    )(hidden, own, peer)


def combine(high, low, blocks):
    tokens, slots = high.shape[0], blocks[0].shape[0]
    rows, width = tokens // Z, blocks[0].shape[1]

    def kernel(high_ref, low_ref, a, b, c, d, near, far, side, corner):
        values = jnp.concatenate([a[...], b[...], c[...], d[...]], axis=0)
        for n, out in enumerate((near, far, side, corner)):
            at = slice(n * rows, (n + 1) * rows)
            total = jnp.dot(high_ref[at], values, preferred_element_type=jnp.float32)
            total += jnp.dot(low_ref[at], values, preferred_element_type=jnp.float32)
            out[...] = total.astype(out.dtype)

    shapes = [
        jax.ShapeDtypeStruct((rows, width), kind)
        for kind in (jnp.float32, jnp.float32, jnp.bfloat16, jnp.bfloat16)
    ]
    return call(
        kernel,
        shapes,
        4 * tokens * X * slots * width,
        X * slots * width * 2 + tokens * width * 3,
    )(high, low, *blocks)


def plan(ids, gates, mine):
    hits = ids[:, :, None] == mine[None, None, :]
    match = jnp.any(hits, axis=1)
    weight = jnp.sum(jnp.where(hits, gates[:, :, None], 0.0), axis=1)
    rank = jnp.cumsum(match.astype(jnp.int32), axis=0) - 1
    capacity = Z * CAP
    here = match[:, :, None] & (rank[:, :, None] == jnp.arange(capacity, dtype=jnp.int32))
    tokens = ids.shape[0]
    one_hot = jnp.transpose(here, (1, 2, 0)).astype(jnp.bfloat16).reshape(X * capacity, tokens)
    spread = jnp.where(here, weight[:, :, None], 0.0).reshape(tokens, X * capacity)
    high = spread.astype(jnp.bfloat16)
    low = (spread - high.astype(jnp.float32)).astype(jnp.bfloat16)
    return one_hot, high, low


def body(rising, falling, gate_up, down_proj, norm_gains, expert_ids, gate_values):
    inputs = (rising[0], falling[0])
    place = lax.axis_index("expert")
    x, half = place // (Z * C), (place // C) % Z // 2
    mine = (x + jnp.arange(X, dtype=jnp.int32)) % X * 2 + half

    normed = [norm(inputs[s], norm_gains[0, s], SENT[s]) for s in range(2)]

    facts = jnp.concatenate(
        [jnp.transpose(expert_ids[0], (0, 2, 1)).astype(jnp.float32), jnp.transpose(gate_values[0], (0, 2, 1))],
        axis=0,
    ).reshape(8, -1)

    def spread_out(block):
        side, far = across_z(block, 1), across_z(block, 2)
        return block, far, side, across_z(far, 1)

    all_facts = [facts, across_z(facts, 2), across_z(facts, 1), across_z(facts, 3)]
    gathered = [[None] * len(SENT[s]) for s in range(2)]
    gathered[0][0] = spread_out(normed[0][0])
    peer_gate_up = across_cores(gate_up)
    peer_down = across_cores(down_proj)
    for s in range(2):
        for n in range(len(SENT[s])):
            if gathered[s][n] is None:
                gathered[s][n] = spread_out(normed[s][n])

    joined = jnp.concatenate(all_facts, axis=1)
    outs = []
    for s in range(2):
        ids = jnp.transpose(joined[2 * s : 2 * s + 2]).astype(jnp.int32)
        gates = jnp.transpose(joined[4 + 2 * s : 6 + 2 * s])
        one_hot, high, low = plan(ids, gates, mine)
        parts = []
        for n in range(len(SENT[s])):
            blocks = dispatch(one_hot, *gathered[s][n])
            parts.append([blocks[0]] + [along_x(blocks[k], k) for k in range(1, X)])
        hidden = gated(parts, gate_up, peer_gate_up, s)
        sent = []
        for at, width in zip(starts(BACK[s]), BACK[s]):
            blocks = lowered(hidden, down_proj, peer_down, s, at, width)
            back = [blocks[0]] + [along_x(blocks[k], -k) for k in range(1, X)]
            near, far, side, corner = combine(high, low, back)
            corner = across_z(corner, 1)
            side = across_z(side, 1)
            far = across_z((far + corner.astype(jnp.float32)).astype(jnp.bfloat16), 2)
            mixture = near + (side.astype(jnp.float32) + far.astype(jnp.float32))
            out = inputs[s][:, at : at + width].astype(jnp.float32) + mixture
            out = out.astype(jnp.bfloat16)
            sent.append((out, shifted(out, 1 - 2 * s)))
        outs.append(sent)
    own = [jnp.concatenate([o for o, _ in sent], axis=1) for sent in outs]
    got = [jnp.concatenate([g for _, g in sent], axis=1) for sent in outs]
    position = lax.axis_index("section")
    final = lax.axis_size("section") - 1
    rising_next = jnp.where(position == 0, own[1], got[0])
    falling_next = jnp.where(position == final, own[0], got[1])
    return (rising_next[None], falling_next[None])


def solution(mesh):
    in_specs = (
        P("section", "expert", None),
        P("section", "expert", None),
        P("section", None, None, None, "expert"),
        P("section", None, "expert", None),
        P("section", None, None),
        P("section", None, "expert", None),
        P("section", None, "expert", None),
    )
    out_specs = (P("section", "expert", None), P("section", "expert", None))
    return jax.shard_map(body, mesh=mesh, in_specs=in_specs, out_specs=out_specs, check_vma=False)
```

```python
import jax
import jax.numpy as jnp
from jax import lax
from jax.experimental import pallas as pl
from jax.experimental.pallas import tpu as pltpu
from jax.sharding import PartitionSpec as P

EPSILON = 1e-06
X, Z, C = 4, 4, 2
CAP = 20
STRIDE = 48
FACTS = 128
UP_TILE, DOWN_TILE = 1792, 1792
PIECE = 512
HALVES = 2


def moved(block, place):
    route = []
    for x in range(X):
        for z in range(Z):
            for c in range(C):
                tx, tz, tc = place(x, z, c)
                route.append(((x * Z + z) * C + c, ((tx % X) * Z + tz) * C + tc))
    return lax.ppermute(block, "expert", route)


def along_x(block, k):
    return moved(block, lambda x, z, c: (x + k, z, c))


def across_z(block, k):
    return moved(block, lambda x, z, c: (x, z ^ k, c))


def across_cores(block):
    return moved(block, lambda x, z, c: (x, z, 1 - c))


def shifted(block, distance):
    devices = range(lax.axis_size("section"))
    route = [(i, i + distance) for i in devices if i + distance in devices]
    return lax.ppermute(block, "section", route)


def after(value, *others):
    return lax.optimization_barrier((value, *others))[0]


def plus(a, b):
    return (a.astype(jnp.float32) + b.astype(jnp.float32)).astype(jnp.bfloat16)


def call(kernel, out_shape, **kw):
    return pl.pallas_call(
        kernel,
        out_shape=out_shape,
        cost_estimate=pl.CostEstimate(flops=1000, bytes_accessed=1000, transcendentals=0),
        compiler_params=pltpu.CompilerParams(vmem_limit_bytes=60 * 1024 * 1024),
        **kw,
    )


def shaped(*shape, kind=jnp.bfloat16):
    return jax.ShapeDtypeStruct(shape, kind)


def iota(shape, dim):
    return lax.broadcasted_iota(jnp.int32, shape, dim)


def dot(a, b, contract=((1,), (0,))):
    return lax.dot_general(a, b, (contract, ((), ())), preferred_element_type=jnp.float32)


def pieces(width):
    return [slice(at, min(at + PIECE, width)) for at in range(0, width, PIECE)]


def normed_of(x, gain):
    x = x.astype(jnp.float32)
    scale = lax.rsqrt(jnp.mean(x * x, axis=-1, keepdims=True) + EPSILON)
    return (x * scale * gain).astype(jnp.bfloat16)


def packed(ids, gates):
    rows = [ids[r : r + 1].astype(jnp.float32) for r in range(2)]
    rest = [gates[r : r + 1] for r in range(2)]
    for _ in range(3):
        terms = [g.astype(jnp.bfloat16).astype(jnp.float32) for g in rest]
        rest = [g - t for g, t in zip(rest, terms)]
        rows += terms
    shape = (8, ids.shape[1])
    total = jnp.zeros(shape, jnp.float32)
    for n, row in enumerate(rows):
        total = jnp.where(iota(shape, 0) == n, jnp.broadcast_to(row, shape), total)
    unit = jnp.where(iota((8, FACTS), 0) == iota((8, FACTS), 1), 1.0, 0.0).astype(jnp.bfloat16)
    return dot(total.astype(jnp.bfloat16), unit, ((0,), (0,))).astype(jnp.bfloat16)


def unpacked(block):
    unit = jnp.where(iota((8, FACTS), 0) == iota((8, FACTS), 1), 1.0, 0.0).astype(jnp.bfloat16)
    rows = dot(unit, block, ((1,), (1,)))
    return [rows[r : r + 1] for r in range(2)] + [
        rows[2 + r : 3 + r] + rows[4 + r : 5 + r] + rows[6 + r : 7 + r] for r in range(2)
    ]


def routes(facts, group, capacity, stride, hot_ref, high_ref, low_ref):
    tokens = facts[0].shape[1]
    count = group * X
    place = lax.axis_index("expert")
    x, half = place // (Z * C), place // (2 * C) % 2
    row = iota((count, tokens), 0)
    if group == 1:
        mine = ((x + row) & (X - 1)) * 2 + half
    else:
        mine = ((x + (row >> 1)) & (X - 1)) * 2 + ((half + row) & 1)
    mine = mine.astype(jnp.float32)
    first, second = facts[0] == mine, facts[1] == mine
    gate = jnp.where(first, facts[2], 0.0) + jnp.where(second, facts[3], 0.0)
    match = jnp.where(first, 1.0, 0.0) + jnp.where(second, 1.0, 0.0)
    until = iota((tokens, tokens), 0) <= iota((tokens, tokens), 1)
    rank = dot(match.astype(jnp.bfloat16), jnp.where(until, 1.0, 0.0).astype(jnp.bfloat16))
    rank = jnp.where(match > 0.0, rank, 0.0)
    shape = (stride, tokens)
    row = iota(shape, 0)
    for k in range(X):
        wanted, weight, slot = (
            jnp.broadcast_to(rank[k * group : k * group + 1], shape),
            jnp.broadcast_to(gate[k * group : k * group + 1], shape),
            row,
        )
        for q in range(1, group):
            e, later = k * group + q, row >= q * capacity
            wanted = jnp.where(later, jnp.broadcast_to(rank[e : e + 1], shape), wanted)
            weight = jnp.where(later, jnp.broadcast_to(gate[e : e + 1], shape), weight)
            slot = jnp.where(later, row - q * capacity, slot)
        slot = jnp.where(row < group * capacity, slot + 1, -1)
        here = wanted == slot.astype(jnp.float32)
        weight = jnp.where(here, weight, 0.0)
        high = weight.astype(jnp.bfloat16)
        at = slice(k * stride, (k + 1) * stride)
        hot_ref[at] = jnp.where(here, 1.0, 0.0).astype(jnp.bfloat16)
        high_ref[at] = high
        low_ref[at] = (weight - high.astype(jnp.float32)).astype(jnp.bfloat16)


def norm_line(values, gains, ids, gates, slot):
    _, rows, width = values.shape

    def kernel(x_ref, gain_ref, ids_ref, gates_ref, out):
        out[:, :width] = normed_of(x_ref[0], gain_ref[0, slot : slot + 1])
        out[:, width:] = packed(ids_ref[0, slot], gates_ref[0, slot])

    return call(kernel, shaped(rows, width + FACTS))(values, gains, ids, gates)


def dispatch_own(values, gains, ids, gates, slot):
    _, rows, width = values.shape

    def kernel(x_ref, gain_ref, ids_ref, gates_ref, *refs):
        outs, (high, low, hot, held) = refs[:X], refs[X:]
        facts = [ids_ref[0, slot, r : r + 1].astype(jnp.float32) for r in range(2)]
        facts += [gates_ref[0, slot, r : r + 1] for r in range(2)]
        routes(facts, 2, CAP, STRIDE, hot, high, low)
        held[...] = normed_of(x_ref[0], gain_ref[0, slot : slot + 1])
        for at in pieces(width):
            value = dot(hot[...], held[:, at]).astype(jnp.bfloat16)
            for k in range(X):
                outs[k][:, at] = value[k * STRIDE : k * STRIDE + 2 * CAP]

    return call(
        kernel,
        [shaped(2 * CAP, width)] * X + [shaped(X * STRIDE, rows)] * 2,
        scratch_shapes=[
            pltpu.VMEM((X * STRIDE, rows), jnp.bfloat16),
            pltpu.VMEM((rows, width), jnp.bfloat16),
        ],
    )(values, gains, ids, gates)


def dispatch_line(blocks):
    rows, width = blocks[0].shape[0], blocks[0].shape[1] - FACTS
    tokens, slots = Z * rows, Z * CAP

    def kernel(*refs):
        ins, outs, (high, low, hot, held) = refs[:Z], refs[Z : Z + X], refs[Z + X :]
        for n in range(Z):
            held[n * rows : (n + 1) * rows] = ins[n][...]
        routes(unpacked(held[:, width:]), 1, slots, slots, hot, high, low)
        for at in pieces(width):
            value = dot(hot[...], held[:, at]).astype(jnp.bfloat16)
            for k in range(X):
                outs[k][:, at] = value[k * slots : (k + 1) * slots]

    return call(
        kernel,
        [shaped(slots, width)] * X + [shaped(X * slots, tokens)] * 2,
        scratch_shapes=[
            pltpu.VMEM((X * slots, tokens), jnp.bfloat16),
            pltpu.VMEM((tokens, width + FACTS), jnp.bfloat16),
        ],
    )(*blocks)


def moves(shape, spans):
    row, column = iota(shape, 0), iota(shape, 1)
    wanted = jnp.full(shape, -1, jnp.int32)
    for to, of, rows in spans:
        wanted = jnp.where((row >= to) & (row < to + rows), row - to + of, wanted)
    return jnp.where(wanted == column, 1.0, 0.0).astype(jnp.bfloat16)


def by_half(blocks):
    slots, width = blocks[0].shape
    half = X * CAP
    spans = [(q * half + k * CAP, k * STRIDE + q * CAP, CAP) for q in range(2) for k in range(X)]

    def kernel(*refs):
        ins, outs, held = refs[:X], refs[X : X + 2], refs[X + 2]
        held[...] = jnp.zeros_like(held)
        for k in range(X):
            held[k * STRIDE : k * STRIDE + slots] = ins[k][...]
        take = moves((2 * half, X * STRIDE), spans)
        for at in pieces(width):
            value = dot(take, held[:, at]).astype(jnp.bfloat16)
            for q in range(2):
                outs[q][:, at] = value[q * half : (q + 1) * half]

    return call(
        kernel,
        [shaped(half, width)] * 2,
        scratch_shapes=[pltpu.VMEM((X * STRIDE, width), jnp.bfloat16)],
    )(*blocks)


def by_column(near, side, far):
    half, width = near.shape
    spans = [(k * STRIDE + q * CAP, q * half + k * CAP, CAP) for q in range(2) for k in range(X)]

    def kernel(near_ref, side_ref, far_ref, *refs):
        outs, held = refs[:X], refs[X]
        held[:half] = plus(near_ref[...], side_ref[...])
        held[half:] = far_ref[...]
        take = moves((X * STRIDE, 2 * half), spans)
        for at in pieces(width):
            value = dot(take, held[:, at]).astype(jnp.bfloat16)
            for k in range(X):
                outs[k][:, at] = value[k * STRIDE : k * STRIDE + 2 * CAP]

    return call(
        kernel,
        [shaped(2 * CAP, width)] * X,
        scratch_shapes=[pltpu.VMEM((2 * half, width), jnp.bfloat16)],
    )(near, side, far)


def experts(blocks, own, own_down, peer, peer_down, slot):
    slots, width = blocks[0].shape
    units = own.shape[4]
    rows = X * slots
    steps, down_steps = width // UP_TILE, width // DOWN_TILE

    def kernel(*refs):
        ins, ups, downs, outs = refs[:X], refs[X : X + 4], refs[X + 4 : X + 6], refs[X + 6 : 2 * X + 6]
        held, acc, hidden = refs[2 * X + 6 :]
        step = pl.program_id(0)

        @pl.when(step < steps)
        def _():
            for k in range(X):
                held[k * slots : (k + 1) * slots] = ins[k][...]
            weight = jnp.concatenate([u[0, 0, 0] for u in ups], axis=1)
            value = dot(held[...], weight)

            @pl.when(step == 0)
            def _():
                acc[...] = value

            @pl.when(step > 0)
            def _():
                acc[...] += value

        @pl.when(step == steps - 1)
        def _():
            for n in range(C):
                gate = acc[:, 2 * n * units : (2 * n + 1) * units]
                value = gate / (1.0 + jnp.exp(-gate)) * acc[:, (2 * n + 1) * units : (2 * n + 2) * units]
                hidden[:, n * units : (n + 1) * units] = value.astype(jnp.bfloat16)

        @pl.when(step >= steps)
        def _():
            weight = jnp.concatenate([d[0, 0] for d in downs], axis=0)
            value = dot(hidden[...], weight).astype(jnp.bfloat16)
            for k in range(X):
                outs[k][...] = value[k * slots : (k + 1) * slots]

    def into(s):
        return jnp.minimum(s, steps - 1)

    def out_of(s):
        return jnp.maximum(s - steps, 0)

    def up(which):
        return pl.BlockSpec((1, 1, 1, UP_TILE, units), lambda s: (0, slot, which, into(s), 0))

    down = pl.BlockSpec((1, 1, units, DOWN_TILE), lambda s: (0, slot, 0, out_of(s)))
    return call(
        kernel,
        [shaped(slots, width)] * X,
        grid=(steps + down_steps,),
        in_specs=[pl.BlockSpec((slots, UP_TILE), lambda s: (0, into(s)))] * X
        + [up(0), up(1), up(0), up(1), down, down],
        out_specs=[pl.BlockSpec((slots, DOWN_TILE), lambda s: (0, out_of(s)))] * X,
        scratch_shapes=[
            pltpu.VMEM((rows, UP_TILE), jnp.bfloat16),
            pltpu.VMEM((rows, 2 * C * units), jnp.float32),
            pltpu.VMEM((rows, C * units), jnp.bfloat16),
        ],
    )(*blocks, own, own, peer, peer, own_down, peer_down)


def combine_own(high, low, blocks, values):
    slots, width = blocks[0].shape
    tokens = high.shape[1]

    def kernel(high_ref, low_ref, *refs):
        ins, x_ref, out, held = refs[:X], refs[X], refs[X + 1], refs[X + 2]
        held[...] = jnp.zeros_like(held)
        for k in range(X):
            held[k * STRIDE : k * STRIDE + slots] = ins[k][...]
        for at in pieces(width):
            mixture = dot(high_ref[...], held[:, at], ((0,), (0,)))
            mixture += dot(low_ref[...], held[:, at], ((0,), (0,)))
            out[:, at] = (x_ref[0, :, at].astype(jnp.float32) + mixture).astype(jnp.bfloat16)

    return call(
        kernel,
        shaped(tokens, width),
        scratch_shapes=[pltpu.VMEM((X * STRIDE, width), jnp.bfloat16)],
    )(high, low, *blocks, values)


def combine_line(high, low, blocks):
    slots, width = blocks[0].shape
    tokens = high.shape[1]
    rows, part = tokens // Z, width // HALVES

    def kernel(high_ref, low_ref, *refs):
        ins, keep, send, held = refs[:X], refs[X : X + 2 * HALVES], refs[-3:-1], refs[-1]
        for k in range(X):
            held[k * slots : (k + 1) * slots] = ins[k][...]
        for h in range(HALVES):
            for at in pieces(part):
                there = slice(h * part + at.start, h * part + at.stop)
                total = dot(high_ref[...], held[:, there], ((0,), (0,)))
                total += dot(low_ref[...], held[:, there], ((0,), (0,)))
                for n in range(2):
                    keep[2 * h + n][:, at] = total[n * rows : (n + 1) * rows]
                    lower = slice((2 + n) * rows, (3 + n) * rows)
                    send[n][:, there] = total[lower].astype(jnp.bfloat16)

    *keep, side, corner = call(
        kernel,
        [shaped(rows, part, kind=jnp.float32)] * (2 * HALVES) + [shaped(rows, width)] * 2,
        scratch_shapes=[pltpu.VMEM((X * slots, width), jnp.bfloat16)],
    )(high, low, *blocks)
    return keep[::2], keep[1::2], side, corner


def body(rising, falling, gate_up, down_proj, norm_gains, expert_ids, gate_values):
    ids, gates = (jnp.transpose(a, (0, 1, 3, 2)) for a in (expert_ids, gate_values))

    normed = norm_line(falling, norm_gains, ids, gates, 1)
    side, far = across_z(normed, 1), across_z(normed, 2)
    peer_up = across_cores(gate_up)
    *own, own_high, own_low = dispatch_own(rising, after(norm_gains, normed), ids, gates, 0)
    own[2] = after(own[2], peer_up)
    own = [own[0]] + [along_x(own[k], k) for k in range(1, X)]
    far = after(far, own[0])
    corner = across_z(far, 1)
    own[0] = after(own[0], far, side)
    near0, far0 = by_half(own)
    peer_down = across_cores(after(down_proj, near0))
    far0 = across_z(after(far0, corner), 2)
    side0 = across_z(after(near0, corner), 1)

    *line, line_high, line_low = dispatch_line([normed, far, side, after(corner, peer_down)])
    far0 = after(far0, line[0], side0)
    rows0 = [near0, far0, side0, across_z(far0, 1)]
    rows1 = [line[0]] + [along_x(line[k], k) for k in range(1, X)]

    line = experts(rows1, gate_up, down_proj, peer_up, peer_down, 1)
    rows0[0] = after(rows0[0], line[0])
    line = [line[0]] + [along_x(line[k], -k) for k in range(1, X)]
    near0, far0, side0, corner0 = experts(rows0, gate_up, down_proj, peer_up, peer_down, 0)
    corner0, side0 = across_z(corner0, 1), across_z(side0, 1)
    near1, far1, side1, corner1 = combine_line(line_high, line_low, line)
    far0 = across_z(plus(far0, after(corner0, near1[0], side0)), 2)
    corner1, side1 = across_z(corner1, 1), across_z(side1, 1)
    width = falling.shape[2] // HALVES
    part = [slice(h * width, (h + 1) * width) for h in range(HALVES)]
    sent1 = [plus(far1[h], corner1[:, part[h]]) for h in range(HALVES)]
    own = by_column(after(near0, sent1[0]), side0, far0)
    own = [own[0]] + [along_x(own[k], -k) for k in range(1, X)]
    far1 = [across_z(sent1[0], 2)]
    far1[0] = after(far1[0], own[0])

    def ended(h):
        mixture = near1[h] + (side1[:, part[h]].astype(jnp.float32) + far1[h].astype(jnp.float32))
        return plus(falling[0, :, part[h]], mixture)

    far1.append(across_z(after(sent1[1], far1[0]), 2))
    out1 = [ended(0)]
    got1 = [shifted(out1[0], -1)]
    own[0] = after(own[0], out1[0])
    out0 = combine_own(own_high, own_low, own, rising)
    got0 = shifted(out0, 1)
    far1[1] = after(far1[1], out0)
    out1.append(ended(1))
    got1.append(shifted(out1[1], -1))
    got1[0] = after(got1[0], got0)
    out1, got1 = jnp.concatenate(out1, axis=1), jnp.concatenate(got1, axis=1)
    position = lax.axis_index("section")
    final = lax.axis_size("section") - 1
    rising_next = jnp.where(position == 0, out1, got0)
    falling_next = jnp.where(position == final, out0, got1)
    return (rising_next[None], falling_next[None])


def solution(mesh):
    in_specs = (
        P("section", "expert", None),
        P("section", "expert", None),
        P("section", None, None, None, "expert"),
        P("section", None, "expert", None),
        P("section", None, None),
        P("section", None, "expert", None),
        P("section", None, "expert", None),
    )
    out_specs = (P("section", "expert", None), P("section", "expert", None))
    return jax.shard_map(body, mesh=mesh, in_specs=in_specs, out_specs=out_specs, check_vma=False)
```

```python
import jax
import jax.numpy as jnp
from jax import lax
from jax.experimental import pallas as pl
from jax.experimental.pallas import tpu as pltpu
from jax.sharding import PartitionSpec as P

EPSILON = 1e-06
X, Z, C = 4, 4, 2
CAP = 20
STRIDE = 48
FACTS = 128
UP_TILE, DOWN_TILE = 1792, 1792
PIECE = 512
HALVES = 2


def moved(block, place):
    route = []
    for x in range(X):
        for z in range(Z):
            for c in range(C):
                tx, tz, tc = place(x, z, c)
                route.append(((x * Z + z) * C + c, ((tx % X) * Z + tz) * C + tc))
    return lax.ppermute(block, "expert", route)


def along_x(block, k):
    return moved(block, lambda x, z, c: (x + k, z, c))


def across_z(block, k):
    return moved(block, lambda x, z, c: (x, z ^ k, c))


def across_cores(block):
    return moved(block, lambda x, z, c: (x, z, 1 - c))


def shifted(block, distance):
    devices = range(lax.axis_size("section"))
    route = [(i, i + distance) for i in devices if i + distance in devices]
    return lax.ppermute(block, "section", route)


def after(value, *others):
    return lax.optimization_barrier((value, *others))[0]


def plus(a, b):
    return (a.astype(jnp.float32) + b.astype(jnp.float32)).astype(jnp.bfloat16)


def call(kernel, out_shape, **kw):
    return pl.pallas_call(
        kernel,
        out_shape=out_shape,
        cost_estimate=pl.CostEstimate(flops=1000, bytes_accessed=1000, transcendentals=0),
        compiler_params=pltpu.CompilerParams(vmem_limit_bytes=60 * 1024 * 1024),
        **kw,
    )


def shaped(*shape, kind=jnp.bfloat16):
    return jax.ShapeDtypeStruct(shape, kind)


def iota(shape, dim):
    return lax.broadcasted_iota(jnp.int32, shape, dim)


def dot(a, b, contract=((1,), (0,))):
    return lax.dot_general(a, b, (contract, ((), ())), preferred_element_type=jnp.float32)


def pieces(width):
    return [slice(at, min(at + PIECE, width)) for at in range(0, width, PIECE)]


def normed_of(x, gain):
    x = x.astype(jnp.float32)
    scale = lax.rsqrt(jnp.mean(x * x, axis=-1, keepdims=True) + EPSILON)
    return (x * scale * gain).astype(jnp.bfloat16)


def packed(ids, gates):
    rows = [ids[r : r + 1].astype(jnp.float32) for r in range(2)]
    rest = [gates[r : r + 1] for r in range(2)]
    for _ in range(3):
        terms = [g.astype(jnp.bfloat16).astype(jnp.float32) for g in rest]
        rest = [g - t for g, t in zip(rest, terms)]
        rows += terms
    shape = (8, ids.shape[1])
    total = jnp.zeros(shape, jnp.float32)
    for n, row in enumerate(rows):
        total = jnp.where(iota(shape, 0) == n, jnp.broadcast_to(row, shape), total)
    unit = jnp.where(iota((8, FACTS), 0) == iota((8, FACTS), 1), 1.0, 0.0).astype(jnp.bfloat16)
    return dot(total.astype(jnp.bfloat16), unit, ((0,), (0,))).astype(jnp.bfloat16)


def unpacked(block):
    unit = jnp.where(iota((8, FACTS), 0) == iota((8, FACTS), 1), 1.0, 0.0).astype(jnp.bfloat16)
    rows = dot(unit, block, ((1,), (1,)))
    return [rows[r : r + 1] for r in range(2)] + [
        rows[2 + r : 3 + r] + rows[4 + r : 5 + r] + rows[6 + r : 7 + r] for r in range(2)
    ]


def routes(facts, group, capacity, stride, hot_ref, weight_ref):
    tokens = facts[0].shape[1]
    count = group * X
    place = lax.axis_index("expert")
    x, half = place // (Z * C), place // (2 * C) % 2
    row = iota((count, tokens), 0)
    if group == 1:
        mine = ((x + row) & (X - 1)) * 2 + half
    else:
        mine = ((x + (row >> 1)) & (X - 1)) * 2 + ((half + row) & 1)
    mine = mine.astype(jnp.float32)
    first, second = facts[0] == mine, facts[1] == mine
    gate = jnp.where(first, facts[2], 0.0) + jnp.where(second, facts[3], 0.0)
    match = jnp.where(first, 1.0, 0.0) + jnp.where(second, 1.0, 0.0)
    until = iota((tokens, tokens), 0) <= iota((tokens, tokens), 1)
    rank = dot(match.astype(jnp.bfloat16), jnp.where(until, 1.0, 0.0).astype(jnp.bfloat16))
    rank = jnp.where(match > 0.0, rank, 0.0)
    shape = (stride, tokens)
    row = iota(shape, 0)
    for k in range(X):
        wanted, weight, slot = (
            jnp.broadcast_to(rank[k * group : k * group + 1], shape),
            jnp.broadcast_to(gate[k * group : k * group + 1], shape),
            row,
        )
        for q in range(1, group):
            e, later = k * group + q, row >= q * capacity
            wanted = jnp.where(later, jnp.broadcast_to(rank[e : e + 1], shape), wanted)
            weight = jnp.where(later, jnp.broadcast_to(gate[e : e + 1], shape), weight)
            slot = jnp.where(later, row - q * capacity, slot)
        slot = jnp.where(row < group * capacity, slot + 1, -1)
        here = wanted == slot.astype(jnp.float32)
        weight = jnp.where(here, weight, 0.0)
        at = slice(k * stride, (k + 1) * stride)
        hot_ref[at] = jnp.where(here, 1.0, 0.0).astype(jnp.bfloat16)
        weight_ref[at] = weight.astype(jnp.bfloat16)


def norm_line(values, gains, ids, gates, slot):
    _, rows, width = values.shape

    def kernel(x_ref, gain_ref, ids_ref, gates_ref, out):
        out[:, :width] = normed_of(x_ref[0], gain_ref[0, slot : slot + 1])
        out[:, width:] = packed(ids_ref[0, slot], gates_ref[0, slot])

    return call(kernel, shaped(rows, width + FACTS))(values, gains, ids, gates)


def dispatch_own(values, gains, ids, gates, slot):
    _, rows, width = values.shape

    def kernel(x_ref, gain_ref, ids_ref, gates_ref, *refs):
        outs, (weights, hot, held) = refs[:X], refs[X:]
        facts = [ids_ref[0, slot, r : r + 1].astype(jnp.float32) for r in range(2)]
        facts += [gates_ref[0, slot, r : r + 1] for r in range(2)]
        routes(facts, 2, CAP, STRIDE, hot, weights)
        held[...] = normed_of(x_ref[0], gain_ref[0, slot : slot + 1])
        for at in pieces(width):
            value = dot(hot[...], held[:, at]).astype(jnp.bfloat16)
            for k in range(X):
                outs[k][:, at] = value[k * STRIDE : k * STRIDE + 2 * CAP]

    return call(
        kernel,
        [shaped(2 * CAP, width)] * X + [shaped(X * STRIDE, rows)],
        scratch_shapes=[
            pltpu.VMEM((X * STRIDE, rows), jnp.bfloat16),
            pltpu.VMEM((rows, width), jnp.bfloat16),
        ],
    )(values, gains, ids, gates)


def dispatch_line(blocks):
    rows, width = blocks[0].shape[0], blocks[0].shape[1] - FACTS
    tokens, slots = Z * rows, Z * CAP

    def kernel(*refs):
        ins, outs, (weights, hot, held) = refs[:Z], refs[Z : Z + X], refs[Z + X :]
        for n in range(Z):
            held[n * rows : (n + 1) * rows] = ins[n][...]
        routes(unpacked(held[:, width:]), 1, slots, slots, hot, weights)
        for at in pieces(width):
            value = dot(hot[...], held[:, at]).astype(jnp.bfloat16)
            for k in range(X):
                outs[k][:, at] = value[k * slots : (k + 1) * slots]

    return call(
        kernel,
        [shaped(slots, width)] * X + [shaped(X * slots, tokens)],
        scratch_shapes=[
            pltpu.VMEM((X * slots, tokens), jnp.bfloat16),
            pltpu.VMEM((tokens, width + FACTS), jnp.bfloat16),
        ],
    )(*blocks)


def moves(shape, spans):
    row, column = iota(shape, 0), iota(shape, 1)
    wanted = jnp.full(shape, -1, jnp.int32)
    for to, of, rows in spans:
        wanted = jnp.where((row >= to) & (row < to + rows), row - to + of, wanted)
    return jnp.where(wanted == column, 1.0, 0.0).astype(jnp.bfloat16)


def by_half(blocks):
    slots, width = blocks[0].shape
    half = X * CAP
    spans = [(q * half + k * CAP, k * STRIDE + q * CAP, CAP) for q in range(2) for k in range(X)]

    def kernel(*refs):
        ins, outs, held = refs[:X], refs[X : X + 2], refs[X + 2]
        held[...] = jnp.zeros_like(held)
        for k in range(X):
            held[k * STRIDE : k * STRIDE + slots] = ins[k][...]
        take = moves((2 * half, X * STRIDE), spans)
        for at in pieces(width):
            value = dot(take, held[:, at]).astype(jnp.bfloat16)
            for q in range(2):
                outs[q][:, at] = value[q * half : (q + 1) * half]

    return call(
        kernel,
        [shaped(half, width)] * 2,
        scratch_shapes=[pltpu.VMEM((X * STRIDE, width), jnp.bfloat16)],
    )(*blocks)


def by_column(near, side, far):
    half, width = near.shape
    spans = [(k * STRIDE + q * CAP, q * half + k * CAP, CAP) for q in range(2) for k in range(X)]

    def kernel(near_ref, side_ref, far_ref, *refs):
        outs, held = refs[:X], refs[X]
        held[:half] = plus(near_ref[...], side_ref[...])
        held[half:] = far_ref[...]
        take = moves((X * STRIDE, 2 * half), spans)
        for at in pieces(width):
            value = dot(take, held[:, at]).astype(jnp.bfloat16)
            for k in range(X):
                outs[k][:, at] = value[k * STRIDE : k * STRIDE + 2 * CAP]

    return call(
        kernel,
        [shaped(2 * CAP, width)] * X,
        scratch_shapes=[pltpu.VMEM((2 * half, width), jnp.bfloat16)],
    )(near, side, far)


def experts(blocks, own, own_down, peer, peer_down, slot):
    slots, width = blocks[0].shape
    units = own.shape[4]
    rows = X * slots
    steps, down_steps = width // UP_TILE, width // DOWN_TILE

    def kernel(*refs):
        ins, ups, downs, outs = refs[:X], refs[X : X + 4], refs[X + 4 : X + 6], refs[X + 6 : 2 * X + 6]
        held, acc, hidden = refs[2 * X + 6 :]
        step = pl.program_id(0)

        @pl.when(step < steps)
        def _():
            for k in range(X):
                held[k * slots : (k + 1) * slots] = ins[k][...]
            weight = jnp.concatenate([u[0, 0, 0] for u in ups], axis=1)
            value = dot(held[...], weight)

            @pl.when(step == 0)
            def _():
                acc[...] = value

            @pl.when(step > 0)
            def _():
                acc[...] += value

        @pl.when(step == steps - 1)
        def _():
            for n in range(C):
                gate = acc[:, 2 * n * units : (2 * n + 1) * units]
                value = gate / (1.0 + jnp.exp(-gate)) * acc[:, (2 * n + 1) * units : (2 * n + 2) * units]
                hidden[:, n * units : (n + 1) * units] = value.astype(jnp.bfloat16)

        @pl.when(step >= steps)
        def _():
            weight = jnp.concatenate([d[0, 0] for d in downs], axis=0)
            value = dot(hidden[...], weight).astype(jnp.bfloat16)
            for k in range(X):
                outs[k][...] = value[k * slots : (k + 1) * slots]

    def into(s):
        return jnp.minimum(s, steps - 1)

    def out_of(s):
        return jnp.maximum(s - steps, 0)

    def up(which):
        return pl.BlockSpec((1, 1, 1, UP_TILE, units), lambda s: (0, slot, which, into(s), 0))

    down = pl.BlockSpec((1, 1, units, DOWN_TILE), lambda s: (0, slot, 0, out_of(s)))
    return call(
        kernel,
        [shaped(slots, width)] * X,
        grid=(steps + down_steps,),
        in_specs=[pl.BlockSpec((slots, UP_TILE), lambda s: (0, into(s)))] * X
        + [up(0), up(1), up(0), up(1), down, down],
        out_specs=[pl.BlockSpec((slots, DOWN_TILE), lambda s: (0, out_of(s)))] * X,
        scratch_shapes=[
            pltpu.VMEM((rows, UP_TILE), jnp.bfloat16),
            pltpu.VMEM((rows, 2 * C * units), jnp.float32),
            pltpu.VMEM((rows, C * units), jnp.bfloat16),
        ],
    )(*blocks, own, own, peer, peer, own_down, peer_down)


def combine_own(weights, blocks, values):
    slots, width = blocks[0].shape
    tokens = weights.shape[1]

    def kernel(weight_ref, *refs):
        ins, x_ref, out, held = refs[:X], refs[X], refs[X + 1], refs[X + 2]
        held[...] = jnp.zeros_like(held)
        for k in range(X):
            held[k * STRIDE : k * STRIDE + slots] = ins[k][...]
        for at in pieces(width):
            mixture = dot(weight_ref[...], held[:, at], ((0,), (0,)))
            out[:, at] = (x_ref[0, :, at].astype(jnp.float32) + mixture).astype(jnp.bfloat16)

    return call(
        kernel,
        shaped(tokens, width),
        scratch_shapes=[pltpu.VMEM((X * STRIDE, width), jnp.bfloat16)],
    )(weights, *blocks, values)


def combine_line(weights, blocks):
    slots, width = blocks[0].shape
    tokens = weights.shape[1]
    rows, part = tokens // Z, width // HALVES

    def kernel(weight_ref, *refs):
        ins, keep, send, held = refs[:X], refs[X : X + 2 * HALVES], refs[-3:-1], refs[-1]
        for k in range(X):
            held[k * slots : (k + 1) * slots] = ins[k][...]
        for h in range(HALVES):
            for at in pieces(part):
                there = slice(h * part + at.start, h * part + at.stop)
                total = dot(weight_ref[...], held[:, there], ((0,), (0,)))
                for n in range(2):
                    keep[2 * h + n][:, at] = total[n * rows : (n + 1) * rows]
                    lower = slice((2 + n) * rows, (3 + n) * rows)
                    send[n][:, there] = total[lower].astype(jnp.bfloat16)

    *keep, side, corner = call(
        kernel,
        [shaped(rows, part, kind=jnp.float32)] * (2 * HALVES) + [shaped(rows, width)] * 2,
        scratch_shapes=[pltpu.VMEM((X * slots, width), jnp.bfloat16)],
    )(weights, *blocks)
    return keep[::2], keep[1::2], side, corner


def body(rising, falling, gate_up, down_proj, norm_gains, expert_ids, gate_values):
    ids, gates = (jnp.transpose(a, (0, 1, 3, 2)) for a in (expert_ids, gate_values))

    normed = norm_line(falling, norm_gains, ids, gates, 1)
    side, far = across_z(normed, 1), across_z(normed, 2)
    peer_up = across_cores(gate_up)
    *own, own_weights = dispatch_own(rising, after(norm_gains, normed), ids, gates, 0)
    own[2] = after(own[2], peer_up)
    own = [own[0]] + [along_x(own[k], k) for k in range(1, X)]
    far = after(far, own[0])
    corner = across_z(far, 1)
    peer_down = across_cores(after(down_proj, far, side, *own[1:]))
    own[0] = after(own[0], peer_down)
    near0, far0 = by_half(own)
    far0 = across_z(after(far0, corner), 2)
    side0 = across_z(after(near0, corner), 1)

    *line, line_weights = dispatch_line([normed, far, side, after(corner, peer_down)])
    far0 = after(far0, line[0], side0)
    rows0 = [near0, far0, side0, across_z(far0, 1)]
    rows1 = [line[0]] + [along_x(line[k], k) for k in range(1, X)]

    line = experts(rows1, gate_up, down_proj, peer_up, peer_down, 1)
    rows0[0] = after(rows0[0], line[0])
    line = [line[0]] + [along_x(line[k], -k) for k in range(1, X)]
    near0, far0, side0, corner0 = experts(rows0, gate_up, down_proj, peer_up, peer_down, 0)
    corner0, side0 = across_z(corner0, 1), across_z(side0, 1)
    near1, far1, side1, corner1 = combine_line(line_weights, line)
    far0 = plus(far0, after(corner0, near1[0], side0))
    corner1, side1 = across_z(corner1, 1), across_z(after(side1, far0), 1)
    far0 = across_z(far0, 2)
    width = falling.shape[2] // HALVES
    part = [slice(h * width, (h + 1) * width) for h in range(HALVES)]
    sent1 = [plus(far1[h], corner1[:, part[h]]) for h in range(HALVES)]
    own = by_column(after(near0, sent1[0]), side0, far0)
    own = [own[0]] + [along_x(own[k], -k) for k in range(1, X)]
    far1 = [across_z(sent1[0], 2)]
    far1[0] = after(far1[0], own[1])

    def ended(h):
        mixture = near1[h] + (side1[:, part[h]].astype(jnp.float32) + far1[h].astype(jnp.float32))
        return plus(falling[0, :, part[h]], mixture)

    far1.append(across_z(after(sent1[1], far1[0]), 2))
    out1 = [ended(0)]
    got1 = [shifted(out1[0], -1)]
    own[0] = after(own[0], out1[0])
    out0 = combine_own(own_weights, own, rising)
    got0 = shifted(out0, 1)
    far1[1] = after(far1[1], out0)
    out1.append(ended(1))
    got1.append(shifted(out1[1], -1))
    got1[0] = after(got1[0], got0)
    out1, got1 = jnp.concatenate(out1, axis=1), jnp.concatenate(got1, axis=1)
    position = lax.axis_index("section")
    final = lax.axis_size("section") - 1
    rising_next = jnp.where(position == 0, out1, got0)
    falling_next = jnp.where(position == final, out0, got1)
    return (rising_next[None], falling_next[None])


def solution(mesh):
    in_specs = (
        P("section", "expert", None),
        P("section", "expert", None),
        P("section", None, None, None, "expert"),
        P("section", None, "expert", None),
        P("section", None, None),
        P("section", None, "expert", None),
        P("section", None, "expert", None),
    )
    out_specs = (P("section", "expert", None), P("section", "expert", None))
    return jax.shard_map(body, mesh=mesh, in_specs=in_specs, out_specs=out_specs, check_vma=False)
```

```python
import jax
import jax.numpy as jnp
from jax import lax
from jax.experimental import pallas as pl
from jax.experimental.pallas import tpu as pltpu
from jax.sharding import PartitionSpec as P

EPSILON = 1e-06
X, Z, C = 4, 4, 2
CAP = 20
STRIDE = 48
FACTS = 128
UP_TILE, DOWN_TILE = 1792, 1792
PIECE = 512
HALVES = 2


def moved(block, place):
    route = []
    for x in range(X):
        for z in range(Z):
            for c in range(C):
                tx, tz, tc = place(x, z, c)
                route.append(((x * Z + z) * C + c, ((tx % X) * Z + tz) * C + tc))
    return lax.ppermute(block, "expert", route)


def along_x(block, k):
    return moved(block, lambda x, z, c: (x + k, z, c))


def across_z(block, k):
    return moved(block, lambda x, z, c: (x, z ^ k, c))


def across_cores(block):
    return moved(block, lambda x, z, c: (x, z, 1 - c))


def shifted(block, distance):
    devices = range(lax.axis_size("section"))
    route = [(i, i + distance) for i in devices if i + distance in devices]
    return lax.ppermute(block, "section", route)


def after(value, *others):
    return lax.optimization_barrier((value, *others))[0]


def plus(a, b):
    return (a.astype(jnp.float32) + b.astype(jnp.float32)).astype(jnp.bfloat16)


def call(kernel, out_shape, **kw):
    return pl.pallas_call(
        kernel,
        out_shape=out_shape,
        cost_estimate=pl.CostEstimate(flops=1000, bytes_accessed=1000, transcendentals=0),
        compiler_params=pltpu.CompilerParams(vmem_limit_bytes=63 * 1024 * 1024 + 512 * 1024),
        **kw,
    )


def shaped(*shape, kind=jnp.bfloat16):
    return jax.ShapeDtypeStruct(shape, kind)


def iota(shape, dim):
    return lax.broadcasted_iota(jnp.int32, shape, dim)


def dot(a, b, contract=((1,), (0,))):
    return lax.dot_general(a, b, (contract, ((), ())), preferred_element_type=jnp.float32)


def pieces(width):
    return [slice(at, min(at + PIECE, width)) for at in range(0, width, PIECE)]


def normed_of(x, gain):
    x = x.astype(jnp.float32)
    scale = lax.rsqrt(jnp.mean(x * x, axis=-1, keepdims=True) + EPSILON)
    return (x * scale * gain).astype(jnp.bfloat16)


def packed(ids, gates):
    rows = [ids[r : r + 1].astype(jnp.float32) for r in range(2)]
    rest = [gates[r : r + 1] for r in range(2)]
    for _ in range(3):
        terms = [g.astype(jnp.bfloat16).astype(jnp.float32) for g in rest]
        rest = [g - t for g, t in zip(rest, terms)]
        rows += terms
    shape = (8, ids.shape[1])
    total = jnp.zeros(shape, jnp.float32)
    for n, row in enumerate(rows):
        total = jnp.where(iota(shape, 0) == n, jnp.broadcast_to(row, shape), total)
    unit = jnp.where(iota((8, FACTS), 0) == iota((8, FACTS), 1), 1.0, 0.0).astype(jnp.bfloat16)
    return dot(total.astype(jnp.bfloat16), unit, ((0,), (0,))).astype(jnp.bfloat16)


def unpacked(block):
    unit = jnp.where(iota((8, FACTS), 0) == iota((8, FACTS), 1), 1.0, 0.0).astype(jnp.bfloat16)
    rows = dot(unit, block, ((1,), (1,)))
    return [rows[r : r + 1] for r in range(2)] + [
        rows[2 + r : 3 + r] + rows[4 + r : 5 + r] + rows[6 + r : 7 + r] for r in range(2)
    ]


def routes(facts, group, capacity, stride, hot_ref, high_ref, low_ref):
    tokens = facts[0].shape[1]
    count = group * X
    place = lax.axis_index("expert")
    x, half = place // (Z * C), place // (2 * C) % 2
    row = iota((count, tokens), 0)
    if group == 1:
        mine = ((x + row) & (X - 1)) * 2 + half
    else:
        mine = ((x + (row >> 1)) & (X - 1)) * 2 + ((half + row) & 1)
    mine = mine.astype(jnp.float32)
    first, second = facts[0] == mine, facts[1] == mine
    gate = jnp.where(first, facts[2], 0.0) + jnp.where(second, facts[3], 0.0)
    match = jnp.where(first, 1.0, 0.0) + jnp.where(second, 1.0, 0.0)
    until = iota((tokens, tokens), 0) <= iota((tokens, tokens), 1)
    rank = dot(match.astype(jnp.bfloat16), jnp.where(until, 1.0, 0.0).astype(jnp.bfloat16))
    rank = jnp.where(match > 0.0, rank, 0.0)
    shape = (stride, tokens)
    row = iota(shape, 0)
    for k in range(X):
        wanted, weight, slot = (
            jnp.broadcast_to(rank[k * group : k * group + 1], shape),
            jnp.broadcast_to(gate[k * group : k * group + 1], shape),
            row,
        )
        for q in range(1, group):
            e, later = k * group + q, row >= q * capacity
            wanted = jnp.where(later, jnp.broadcast_to(rank[e : e + 1], shape), wanted)
            weight = jnp.where(later, jnp.broadcast_to(gate[e : e + 1], shape), weight)
            slot = jnp.where(later, row - q * capacity, slot)
        slot = jnp.where(row < group * capacity, slot + 1, -1)
        here = wanted == slot.astype(jnp.float32)
        weight = jnp.where(here, weight, 0.0)
        high = weight.astype(jnp.bfloat16)
        at = slice(k * stride, (k + 1) * stride)
        hot_ref[at] = jnp.where(here, 1.0, 0.0).astype(jnp.bfloat16)
        high_ref[at] = high
        low_ref[at] = (weight - high.astype(jnp.float32)).astype(jnp.bfloat16)


def norm_line(values, gains, ids, gates, slot):
    _, rows, width = values.shape

    def kernel(x_ref, gain_ref, ids_ref, gates_ref, out):
        out[:, :width] = normed_of(x_ref[0], gain_ref[0, slot : slot + 1])
        out[:, width:] = packed(ids_ref[0, slot], gates_ref[0, slot])

    return call(kernel, shaped(rows, width + FACTS))(values, gains, ids, gates)


def dispatch_own(values, gains, ids, gates, slot):
    _, rows, width = values.shape

    def kernel(x_ref, gain_ref, ids_ref, gates_ref, *refs):
        outs, (high, low, hot, held) = refs[:X], refs[X:]
        facts = [ids_ref[0, slot, r : r + 1].astype(jnp.float32) for r in range(2)]
        facts += [gates_ref[0, slot, r : r + 1] for r in range(2)]
        routes(facts, 2, CAP, STRIDE, hot, high, low)
        held[...] = normed_of(x_ref[0], gain_ref[0, slot : slot + 1])
        for at in pieces(width):
            value = dot(hot[...], held[:, at]).astype(jnp.bfloat16)
            for k in range(X):
                outs[k][:, at] = value[k * STRIDE : k * STRIDE + 2 * CAP]

    return call(
        kernel,
        [shaped(2 * CAP, width)] * X + [shaped(X * STRIDE, rows)] * 2,
        scratch_shapes=[
            pltpu.VMEM((X * STRIDE, rows), jnp.bfloat16),
            pltpu.VMEM((rows, width), jnp.bfloat16),
        ],
    )(values, gains, ids, gates)


def dispatch_line(blocks):
    rows, width = blocks[0].shape[0], blocks[0].shape[1] - FACTS
    tokens, slots = Z * rows, Z * CAP

    def kernel(*refs):
        ins, outs, (high, low, hot, held) = refs[:Z], refs[Z : Z + X], refs[Z + X :]
        for n in range(Z):
            held[n * rows : (n + 1) * rows] = ins[n][...]
        routes(unpacked(held[:, width:]), 1, slots, slots, hot, high, low)
        for at in pieces(width):
            value = dot(hot[...], held[:, at]).astype(jnp.bfloat16)
            for k in range(X):
                outs[k][:, at] = value[k * slots : (k + 1) * slots]

    return call(
        kernel,
        [shaped(slots, width)] * X + [shaped(X * slots, tokens)] * 2,
        scratch_shapes=[
            pltpu.VMEM((X * slots, tokens), jnp.bfloat16),
            pltpu.VMEM((tokens, width + FACTS), jnp.bfloat16),
        ],
    )(*blocks)


def moves(shape, spans):
    row, column = iota(shape, 0), iota(shape, 1)
    wanted = jnp.full(shape, -1, jnp.int32)
    for to, of, rows in spans:
        wanted = jnp.where((row >= to) & (row < to + rows), row - to + of, wanted)
    return jnp.where(wanted == column, 1.0, 0.0).astype(jnp.bfloat16)


def by_half(blocks):
    slots, width = blocks[0].shape
    half = X * CAP
    spans = [(q * half + k * CAP, k * STRIDE + q * CAP, CAP) for q in range(2) for k in range(X)]

    def kernel(*refs):
        ins, outs, held = refs[:X], refs[X : X + 2], refs[X + 2]
        held[...] = jnp.zeros_like(held)
        for k in range(X):
            held[k * STRIDE : k * STRIDE + slots] = ins[k][...]
        take = moves((2 * half, X * STRIDE), spans)
        for at in pieces(width):
            value = dot(take, held[:, at]).astype(jnp.bfloat16)
            for q in range(2):
                outs[q][:, at] = value[q * half : (q + 1) * half]

    return call(
        kernel,
        [shaped(half, width)] * 2,
        scratch_shapes=[pltpu.VMEM((X * STRIDE, width), jnp.bfloat16)],
    )(*blocks)


def by_column(near, side, far):
    half, width = near.shape
    spans = [(k * STRIDE + q * CAP, q * half + k * CAP, CAP) for q in range(2) for k in range(X)]

    def kernel(near_ref, side_ref, far_ref, *refs):
        outs, held = refs[:X], refs[X]
        held[:half] = plus(near_ref[...], side_ref[...])
        held[half:] = far_ref[...]
        take = moves((X * STRIDE, 2 * half), spans)
        for at in pieces(width):
            value = dot(take, held[:, at]).astype(jnp.bfloat16)
            for k in range(X):
                outs[k][:, at] = value[k * STRIDE : k * STRIDE + 2 * CAP]

    return call(
        kernel,
        [shaped(2 * CAP, width)] * X,
        scratch_shapes=[pltpu.VMEM((2 * half, width), jnp.bfloat16)],
    )(near, side, far)


def experts(blocks, own, own_down, peer, peer_down, slot):
    slots, width = blocks[0].shape
    units = own.shape[4]
    rows = X * slots
    steps, down_steps = width // UP_TILE, width // DOWN_TILE

    def kernel(*refs):
        ins, ups, downs, outs = refs[:X], refs[X : X + 4], refs[X + 4 : X + 6], refs[X + 6 : 2 * X + 6]
        held, acc, hidden = refs[2 * X + 6 :]
        step = pl.program_id(0)

        @pl.when(step < steps)
        def _():
            for k in range(X):
                held[k * slots : (k + 1) * slots] = ins[k][...]
            weight = jnp.concatenate([u[0, 0, 0] for u in ups], axis=1)
            value = dot(held[...], weight)

            @pl.when(step == 0)
            def _():
                acc[...] = value

            @pl.when(step > 0)
            def _():
                acc[...] += value

        @pl.when(step == steps - 1)
        def _():
            for n in range(C):
                gate = acc[:, 2 * n * units : (2 * n + 1) * units]
                value = gate / (1.0 + jnp.exp(-gate)) * acc[:, (2 * n + 1) * units : (2 * n + 2) * units]
                hidden[:, n * units : (n + 1) * units] = value.astype(jnp.bfloat16)

        @pl.when(step >= steps)
        def _():
            weight = jnp.concatenate([d[0, 0] for d in downs], axis=0)
            value = dot(hidden[...], weight).astype(jnp.bfloat16)
            for k in range(X):
                outs[k][...] = value[k * slots : (k + 1) * slots]

    def into(s):
        return jnp.minimum(s, steps - 1)

    def out_of(s):
        return jnp.maximum(s - steps, 0)

    def up(which):
        return pl.BlockSpec((1, 1, 1, UP_TILE, units), lambda s: (0, slot, which, into(s), 0))

    down = pl.BlockSpec((1, 1, units, DOWN_TILE), lambda s: (0, slot, 0, out_of(s)))
    return call(
        kernel,
        [shaped(slots, width)] * X,
        grid=(steps + down_steps,),
        in_specs=[pl.BlockSpec((slots, UP_TILE), lambda s: (0, into(s)))] * X
        + [up(0), up(1), up(0), up(1), down, down],
        out_specs=[pl.BlockSpec((slots, DOWN_TILE), lambda s: (0, out_of(s)))] * X,
        scratch_shapes=[
            pltpu.VMEM((rows, UP_TILE), jnp.bfloat16),
            pltpu.VMEM((rows, 2 * C * units), jnp.float32),
            pltpu.VMEM((rows, C * units), jnp.bfloat16),
        ],
    )(*blocks, own, own, peer, peer, own_down, peer_down)


def combine_own(high, low, blocks, values):
    slots, width = blocks[0].shape
    tokens = high.shape[1]

    def kernel(high_ref, low_ref, *refs):
        ins, x_ref, out, held = refs[:X], refs[X], refs[X + 1], refs[X + 2]
        held[...] = jnp.zeros_like(held)
        for k in range(X):
            held[k * STRIDE : k * STRIDE + slots] = ins[k][...]
        for at in pieces(width):
            mixture = dot(high_ref[...], held[:, at], ((0,), (0,)))
            mixture += dot(low_ref[...], held[:, at], ((0,), (0,)))
            out[:, at] = (x_ref[0, :, at].astype(jnp.float32) + mixture).astype(jnp.bfloat16)

    return call(
        kernel,
        shaped(tokens, width),
        scratch_shapes=[pltpu.VMEM((X * STRIDE, width), jnp.bfloat16)],
    )(high, low, *blocks, values)


def combine_line(high, low, blocks):
    slots, width = blocks[0].shape
    tokens = high.shape[1]
    rows, part = tokens // Z, width // HALVES

    def kernel(high_ref, low_ref, *refs):
        ins, keep, send, held = refs[:X], refs[X : X + 2 * HALVES], refs[-3:-1], refs[-1]
        for k in range(X):
            held[k * slots : (k + 1) * slots] = ins[k][...]
        for h in range(HALVES):
            for at in pieces(part):
                there = slice(h * part + at.start, h * part + at.stop)
                total = dot(high_ref[...], held[:, there], ((0,), (0,)))
                total += dot(low_ref[...], held[:, there], ((0,), (0,)))
                for n in range(2):
                    keep[2 * h + n][:, at] = total[n * rows : (n + 1) * rows]
                    lower = slice((2 + n) * rows, (3 + n) * rows)
                    send[n][:, there] = total[lower].astype(jnp.bfloat16)

    *keep, side, corner = call(
        kernel,
        [shaped(rows, part, kind=jnp.float32)] * (2 * HALVES) + [shaped(rows, width)] * 2,
        scratch_shapes=[pltpu.VMEM((X * slots, width), jnp.bfloat16)],
    )(high, low, *blocks)
    return keep[::2], keep[1::2], side, corner


def body(rising, falling, gate_up, down_proj, norm_gains, expert_ids, gate_values):
    ids, gates = (jnp.transpose(a, (0, 1, 3, 2)) for a in (expert_ids, gate_values))

    normed = norm_line(falling, norm_gains, ids, gates, 1)
    side, far = across_z(normed, 1), across_z(normed, 2)
    peer_up = across_cores(gate_up)
    *own, own_high, own_low = dispatch_own(rising, after(norm_gains, normed), ids, gates, 0)
    own[2] = after(own[2], peer_up)
    own = [own[0]] + [along_x(own[k], k) for k in range(1, X)]
    far = after(far, own[0])
    corner = across_z(far, 1)
    own[0] = after(own[0], far, side)
    near0, far0 = by_half(own)
    peer_down = across_cores(after(down_proj, near0))
    far0 = across_z(after(far0, corner), 2)
    side0 = across_z(after(near0, corner), 1)

    *line, line_high, line_low = dispatch_line([normed, far, side, after(corner, peer_down)])
    far0 = after(far0, line[0], side0)
    rows0 = [near0, far0, side0, across_z(far0, 1)]
    rows1 = [line[0]] + [along_x(line[k], k) for k in range(1, X)]

    line = experts(rows1, gate_up, down_proj, peer_up, peer_down, 1)
    rows0[0] = after(rows0[0], line[0])
    line = [line[0]] + [along_x(line[k], -k) for k in range(1, X)]
    near0, far0, side0, corner0 = experts(rows0, gate_up, down_proj, peer_up, peer_down, 0)
    corner0, side0 = across_z(corner0, 1), across_z(side0, 1)
    near1, far1, side1, corner1 = combine_line(line_high, line_low, line)
    far0 = across_z(plus(far0, after(corner0, near1[0], side0)), 2)
    corner1, side1 = across_z(corner1, 1), across_z(side1, 1)
    width = falling.shape[2] // HALVES
    part = [slice(h * width, (h + 1) * width) for h in range(HALVES)]
    sent1 = [plus(far1[h], corner1[:, part[h]]) for h in range(HALVES)]
    own = by_column(after(near0, sent1[0]), side0, far0)
    own = [own[0]] + [along_x(own[k], -k) for k in range(1, X)]
    far1 = [across_z(sent1[0], 2)]
    far1[0] = after(far1[0], own[0])

    def ended(h):
        mixture = near1[h] + (side1[:, part[h]].astype(jnp.float32) + far1[h].astype(jnp.float32))
        return plus(falling[0, :, part[h]], mixture)

    far1.append(across_z(after(sent1[1], far1[0]), 2))
    out1 = [ended(0)]
    got1 = [shifted(out1[0], -1)]
    own[0] = after(own[0], out1[0])
    out0 = combine_own(own_high, own_low, own, rising)
    got0 = shifted(out0, 1)
    far1[1] = after(far1[1], out0)
    out1.append(ended(1))
    got1.append(shifted(out1[1], -1))
    got1[0] = after(got1[0], got0)
    out1, got1 = jnp.concatenate(out1, axis=1), jnp.concatenate(got1, axis=1)
    position = lax.axis_index("section")
    final = lax.axis_size("section") - 1
    rising_next = jnp.where(position == 0, out1, got0)
    falling_next = jnp.where(position == final, out0, got1)
    return (rising_next[None], falling_next[None])


def solution(mesh):
    in_specs = (
        P("section", "expert", None),
        P("section", "expert", None),
        P("section", None, None, None, "expert"),
        P("section", None, "expert", None),
        P("section", None, None),
        P("section", None, "expert", None),
        P("section", None, "expert", None),
    )
    out_specs = (P("section", "expert", None), P("section", "expert", None))
    return jax.shard_map(body, mesh=mesh, in_specs=in_specs, out_specs=out_specs, check_vma=False)
```
